256 devices in a mesh: expert: 64 (over x, z, core), dp: 4 (over y).
Axes of the slice: x: 4, y: 4, z: 8, core: 2. Of those that a mesh axis runs over, the one named last changes fastest.
Arguments:
- tokens: bfloat16 [8192, 4096], P('expert'), may hold values from -6 to 6
- cotangent: bfloat16 [8192, 4096], P('expert'), may hold values from -6 to 6
- gates: float32 [8192, 2], P('expert'), may hold values from 0.2 to 1
- routing: int32 [8192, 2], P('expert'), may hold values from 0 to 31, all different within a row; in each aligned block of 128 rows (0 to 127, 128 to 255, ...) at most 16 rows name the same one
- gate_weight: bfloat16 [64, 768, 4096], P('expert', 'dp'), may hold values from -0.09375 to 0.09375
- up_weight: bfloat16 [64, 768, 4096], P('expert', 'dp'), may hold values from -0.09375 to 0.09375
- down_weight: bfloat16 [64, 768, 4096], P('expert', 'dp'), may hold values from -0.15625 to 0.15625
Outputs:
- input_grad: bfloat16 [8192, 4096], P('expert', 'dp')
- gate_grad: bfloat16 [64, 768, 4096], P('expert', 'dp')
- up_grad: bfloat16 [64, 768, 4096], P('expert', 'dp')
- down_grad: bfloat16 [64, 768, 4096], P('expert', 'dp')
The draws below stay inside these ranges and needn't reach their ends.
Inputs may be any that keep to these rules, and one draw needn't show every extreme that they name: `routing`: each row names 2 different experts. Among the 128 rows of one token group (aligned blocks) no expert is named by more than 16 rows, a bound that some block reaches.
All inputs are finite; a program needn't handle non-finite values.
Results may differ from the reference program's by a relative error of at most 0.012.
Values may be sent and summed in bfloat16 or wider, within the bound.
No kernel may reach another device: no remote copies, remote signals or barrier semaphores. Data moves between devices by JAX's collectives and lax.ppermute only.
A program may use at most 128 MiB of HBM per device.

```python
import math
import jax
import jax.numpy as jnp
import numpy as np
from jax import lax

D = 4096
FF = 1536
TOK_DEV = 128
TOP = 2
EXPERTS = 32
CAP = 16
HALF = 768
SLICE = 192
TOKENS = 8192
N_EXPERT = 64
N_DP = 4


def shard_levels(stream_key, extent, shards, low, top_value):
    gain, own = 1.0, jax.random.fold_in(stream_key, 6)
    for dim, blocks in shards:
        steps = jnp.exp(jax.random.uniform(jax.random.fold_in(own, dim), (blocks,), jnp.float32, low / len(shards), top_value / len(shards)))
        gain = gain * jnp.repeat(steps, extent[dim] // blocks).reshape([-1 if axis == dim else 1 for axis in range(len(extent))])
    return gain


def deal_out(stream_key, own, number, rows, count, top, reach, skew):
    order = jax.random.permutation(stream_key, count)
    packed, usual = shares(count, rows * top, reach, skew, True), shares(count, rows * top, reach, skew, False)
    places = jnp.arange(count)

    def named(lengths, turn):
        used = int((lengths > 0).sum())
        fixed = max(1, used // 4)
        passed = fixed + (places - fixed + turn * (used - fixed)) % max(1, count - fixed)
        return jnp.zeros((count,), jnp.int32).at[order[jnp.where(places < fixed, places, passed)]].set(jnp.asarray(lengths, jnp.int32))

    lengths = jnp.where(number % 4 == 0, named(packed, number // 4), named(usual, number - number // 4 - 1))
    mixed = jax.random.permutation(jax.random.fold_in(own, 3), count)
    donor, taker = mixed[0:count // 2 * 2:2], mixed[1:count // 2 * 2:2]
    room = jnp.minimum(lengths[donor] - 1, reach - lengths[taker]) // 2
    room = jnp.where((donor == order[0]) | (taker == order[0]) | (lengths[taker] == 0), 0, jnp.maximum(room, 0))
    passed = jax.random.randint(jax.random.fold_in(own, 4), (count // 2,), 0, 1 << 20) % (room + 1)
    lengths = lengths.at[donor].add(-passed).at[taker].add(passed)
    labels = jnp.searchsorted(jnp.cumsum(lengths), jnp.arange(rows * top), side="right").astype(jnp.int32)
    grid = labels.reshape(top, rows).T
    grid = grid[jax.random.permutation(jax.random.fold_in(own, 1), rows)]
    turn = jax.random.randint(jax.random.fold_in(own, 2), (rows, 1), 0, top)
    return jnp.take_along_axis(grid, (jnp.arange(top)[None, :] + turn) % top, axis=1)


def shares(count, total, bound, skew, full):
    loads = [(1 << 20) // math.isqrt(rank ** skew) + 1 for rank in range(1, count + 1)]
    largest = bound if full else min(bound, max(-(-total // count), total * loads[0] // sum(loads)))
    least = 1 if total - largest >= count - 1 else 0
    holding, spare = [largest] + [least] * (count - 1), total - largest - least * (count - 1)
    while spare > 0:
        candidates = [i for i in range(1, count) if holding[i] < largest] or [i for i in range(1, count) if holding[i] < bound]
        pool, budget = sum([loads[i] for i in candidates]), spare
        for i in candidates:
            addition = min(bound - holding[i], max(1, budget * loads[i] // pool), spare)
            holding[i] = holding[i] + addition
            spare = spare - addition
    return np.array(holding)


def bell_draw(own_key, dims, deviation, bound, shards=(), kind=jnp.bfloat16):
    gain = shard_levels(own_key, dims, shards, -0.22, 0.18) if shards else 1.0
    drawn = jax.random.normal(own_key, dims, jnp.float32) * deviation * gain
    return jnp.minimum(jnp.maximum(drawn, -bound), bound).astype(kind)


def setup_inputs(seed: int = 0) -> dict:
    key_of = jax.random.split(jax.random.key(seed), 8)
    tokens = bell_draw(key_of[0], (TOKENS, D), 1.0, 6.0, ((0, 64),))
    cotangent = bell_draw(key_of[1], (TOKENS, D), 1.0, 6.0, ((0, 64),))
    gates = jnp.clip(0.2 + 0.8 * jax.random.uniform(key_of[2], (TOKENS, TOP), jnp.float32) ** shard_levels(key_of[2], (TOKENS, TOP), ((0, 64),), -0.2, 0.2), 0.2, 1.0)
    routing_keys = jax.random.split(jax.random.fold_in(key_of[3], 1), TOKENS // TOK_DEV)
    routing_turns = jax.random.permutation(jax.random.fold_in(key_of[3], 3), TOKENS // TOK_DEV)
    routing = jax.vmap(lambda own, number: deal_out(jax.random.fold_in(key_of[3], 2), own, number, TOK_DEV, EXPERTS, TOP, CAP, 2))(routing_keys, routing_turns).reshape((TOKENS, TOP))
    gate_weight = bell_draw(key_of[4], (2 * EXPERTS, HALF, D), D ** -0.5, 0.09375, ((0, 64), (1, 4)))
    up_weight = bell_draw(key_of[5], (2 * EXPERTS, HALF, D), D ** -0.5, 0.09375, ((0, 64), (1, 4)))
    down_weight = bell_draw(key_of[6], (2 * EXPERTS, HALF, D), FF ** -0.5, 0.15625, ((0, 64), (1, 4)))
    return {"tokens": tokens, "cotangent": cotangent, "gates": gates, "routing": routing, "gate_weight": gate_weight, "up_weight": up_weight, "down_weight": down_weight}


def reference(tokens, cotangent, gates, routing, gate_weight, up_weight, down_weight):
    per_group = TOK_DEV * TOP
    blocks = 2 * N_DP
    flat_routes = routing.reshape(N_EXPERT, per_group)
    onehot = (flat_routes[:, :, None] == jnp.arange(EXPERTS, dtype=jnp.int32)[None, None, :]).astype(jnp.int32)
    ranks = jnp.sum((jnp.cumsum(onehot, axis=1) - 1) * onehot, axis=2).astype(jnp.int32)
    groups = jnp.arange(N_EXPERT, dtype=jnp.int32)[:, None]
    places = (flat_routes * (N_EXPERT * CAP) + groups * CAP + ranks).reshape(-1)
    ident = jnp.arange(N_EXPERT * per_group, dtype=jnp.int32)
    filler = jnp.zeros((EXPERTS * N_EXPERT * CAP,), jnp.int32).at[places].set(ident + 1)
    filler = filler.reshape(EXPERTS, N_EXPERT * CAP)
    gate_flat = gates.reshape(-1)
    contract_rows = (((0,), (0,)), ((), ()))
    contract_cols = (((1,), (1,)), ((), ()))

    def expert_step(carry, index):
        entry = filler[index]
        live = entry > 0
        route = jnp.maximum(entry - 1, 0)
        token = (route // TOP).astype(jnp.int32)
        rows_x = jnp.where(live[:, None], tokens[token], jnp.zeros((), tokens.dtype))
        scaled_full = gate_flat[route][:, None] * cotangent[token].astype(jnp.float32)
        rows_g = jnp.where(live[:, None], scaled_full, jnp.zeros((), jnp.float32)).astype(jnp.bfloat16)
        w_gate = lax.dynamic_slice_in_dim(gate_weight, 2 * index, 2, 0).reshape(FF, D)
        w_up = lax.dynamic_slice_in_dim(up_weight, 2 * index, 2, 0).reshape(FF, D)
        w_down = lax.dynamic_slice_in_dim(down_weight, 2 * index, 2, 0).reshape(FF, D)
        gate = lax.dot_general(rows_x, w_gate, contract_cols, preferred_element_type=jnp.float32)
        upval = lax.dot_general(rows_x, w_up, contract_cols, preferred_element_type=jnp.float32)
        sigma = jax.nn.sigmoid(gate)
        active = gate * sigma
        hidden = (active * upval).astype(jnp.bfloat16)
        dhid = lax.dot_general(rows_g, w_down, contract_cols, preferred_element_type=jnp.float32)
        dgate = (dhid * upval * sigma * (1.0 + gate * (1.0 - sigma))).astype(jnp.bfloat16)
        dup = (dhid * active).astype(jnp.bfloat16)
        grad_down = lax.dot_general(hidden, rows_g, contract_rows, preferred_element_type=jnp.float32).astype(jnp.bfloat16)
        grad_gate = lax.dot_general(dgate, rows_x, contract_rows, preferred_element_type=jnp.float32).astype(jnp.bfloat16)
        grad_up = lax.dot_general(dup, rows_x, contract_rows, preferred_element_type=jnp.float32).astype(jnp.bfloat16)
        count = rows_x.shape[0]
        terms = jnp.einsum('rbs,bsd->brd', dgate.astype(jnp.float32).reshape(count, blocks, SLICE),
                           w_gate.astype(jnp.float32).reshape(blocks, SLICE, D))
        terms = terms + jnp.einsum('rbs,bsd->brd', dup.astype(jnp.float32).reshape(count, blocks, SLICE),
                                   w_up.astype(jnp.float32).reshape(blocks, SLICE, D))
        rounded = lax.optimization_barrier(terms.astype(jnp.bfloat16))
        total = jnp.sum(rounded.astype(jnp.float32), axis=0)
        target = jnp.where(live, token, TOKENS).astype(jnp.int32)
        carry = carry.at[target].add(total)
        grad_gate = grad_gate.reshape(2, HALF, D)
        grad_up = grad_up.reshape(2, HALF, D)
        grad_down = grad_down.reshape(2, HALF, D)
        return carry, (grad_gate, grad_up, grad_down)

    start = jnp.zeros((TOKENS + 1, D), jnp.float32)
    final, stacked = lax.scan(expert_step, start, jnp.arange(EXPERTS, dtype=jnp.int32))
    gate_grad = stacked[0].reshape(2 * EXPERTS, HALF, D)
    up_grad = stacked[1].reshape(2 * EXPERTS, HALF, D)
    down_grad = stacked[2].reshape(2 * EXPERTS, HALF, D)
    input_grad = final[:TOKENS].astype(jnp.bfloat16)
    return (input_grad, gate_grad, up_grad, down_grad)
```

```python
import functools

import jax
import jax.numpy as jnp
from jax import lax
from jax.experimental import pallas as pl
from jax.experimental.pallas import tpu as pltpu
from jax.sharding import PartitionSpec as P

F32 = jnp.float32
BF16 = jnp.bfloat16
NT = (((1,), (1,)), ((), ()))
TN = (((0,), (0,)), ((), ()))
VMEM = pl.BlockSpec(memory_space=pltpu.VMEM)
PARAMS = pltpu.CompilerParams(vmem_limit_bytes=60 * 1024 * 1024)


def dot(a, b, dims=(((1,), (0,)), ((), ()))):
    return lax.dot_general(a, b, dims, preferred_element_type=F32)


def slot_places(routing_ref, experts, capacity):
    tok = routing_ref.shape[1]
    ids = lax.broadcasted_iota(jnp.int32, (experts, tok), 0)
    first, second = routing_ref[0:1, :], routing_ref[1:2, :]
    hot0 = jnp.where(ids == first, 1.0, 0.0).astype(F32)
    hot1 = jnp.where(ids == second, 1.0, 0.0).astype(F32)
    row = lax.broadcasted_iota(jnp.int32, (tok, tok), 0)
    col = lax.broadcasted_iota(jnp.int32, (tok, tok), 1)
    before = jnp.where(row < col, 1.0, 0.0).astype(BF16)
    count0 = dot(hot0.astype(BF16), before)
    count1 = dot(hot1.astype(BF16), before) + jnp.sum(hot0, axis=1, keepdims=True)
    rank0 = jnp.sum(hot0 * count0, axis=0, keepdims=True).astype(jnp.int32)
    rank1 = jnp.sum(hot1 * count1, axis=0, keepdims=True).astype(jnp.int32)
    return first * capacity + rank0, second * capacity + rank1


def slot_masks(routing_ref, experts, capacity):
    tok = routing_ref.shape[1]
    place0, place1 = slot_places(routing_ref, experts, capacity)
    slots = lax.broadcasted_iota(jnp.int32, (experts * capacity, tok), 0)
    return (
        jnp.where(slots == place0, 1.0, 0.0).astype(BF16),
        jnp.where(slots == place1, 1.0, 0.0).astype(BF16),
    )


def build_x(experts, capacity, idx_ref, routing_ref, tok_ref, out_ref):
    mask0, mask1 = slot_masks(routing_ref, experts, capacity)
    half = tok_ref.shape[1] // 2
    for c in range(2):
        rows = dot(mask0 + mask1, tok_ref[:, c * half : (c + 1) * half])
        out_ref[:, c] = rows.astype(BF16).reshape(experts, capacity, half)


def build_g(experts, capacity, idx_ref, routing_ref, gates_ref, cot_ref, out_ref):
    mask0, mask1 = slot_masks(routing_ref, experts, capacity)
    half = cot_ref.shape[1] // 2
    for c in range(2):
        cot = cot_ref[:, c * half : (c + 1) * half].astype(F32)
        rows = dot(mask0, (gates_ref[:, 0:1] * cot).astype(BF16))
        rows = rows + dot(mask1, (gates_ref[:, 1:2] * cot).astype(BF16))
        out_ref[:, c] = rows.astype(BF16).reshape(experts, capacity, half)


def combine(experts, capacity, routing_ref, back_ref, out_ref):
    mask0, mask1 = slot_masks(routing_ref, experts, capacity)
    half = back_ref.shape[3]
    for c in range(2):
        rows = back_ref[:, c].reshape(experts * capacity, half)
        out_ref[:, c * half : (c + 1) * half] = dot(mask0 + mask1, rows, TN).astype(BF16)


def columns(idx_ref, place, width):
    return pl.ds(pl.multiple_of(idx_ref[place] * width, width), width)


def over_rows(total, tile, body):
    for half in range(2):

        @pl.loop(0, total // 2 // tile)
        def _(i, half=half):
            here = pl.multiple_of(i * tile, tile)
            body(half, pl.ds(pl.multiple_of(half * (total // 2) + here, tile), tile), pl.ds(here, tile))


def pick(refs, core, place, half):
    group = refs[core * 5 : core * 5 + 5]
    return group[place] if place < 3 else group[3 + half]


def gate_up(idx_ref, *refs):
    xs, (wg, wu, gate_ref, up_ref) = refs[:10], refs[10:]
    width = xs[0].shape[1]

    def body(half, rows, local):
        gate = up = None
        for core in range(2):
            for place in range(4):
                x = pick(xs, core, place, half)[rows if place < 3 else local, :]
                cols = columns(idx_ref, core * 4 + place, width)
                a, b = dot(x, wg[:, cols], NT), dot(x, wu[:, cols], NT)
                gate, up = (a, b) if gate is None else (gate + a, up + b)
        gate_ref[rows, :] = gate
        up_ref[rows, :] = up

    over_rows(xs[0].shape[0], 256, body)


def middle(idx_ref, *refs):
    gs, (wd, gate_ref, up_ref, hidden_ref, dgate_ref, dup_ref) = refs[:10], refs[10:]
    width = gs[0].shape[1]

    def body(half, rows, local):
        dhid = None
        for core in range(2):
            for place in range(4):
                g = pick(gs, core, place, half)[rows if place < 3 else local, :]
                a = dot(g, wd[:, columns(idx_ref, core * 4 + place, width)], NT)
                dhid = a if dhid is None else dhid + a
        gate, up = gate_ref[rows, :], up_ref[rows, :]
        sigma = jax.nn.sigmoid(gate)
        active = gate * sigma
        hidden_ref[rows, :] = (active * up).astype(BF16)
        dgate_ref[rows, :] = (dhid * up * sigma * (1.0 + gate * (1.0 - sigma))).astype(BF16)
        dup_ref[rows, :] = (dhid * active).astype(BF16)

    over_rows(gs[0].shape[0], 256, body)


def term_block(idx_ref, dgate_ref, dup_ref, wg, wu, out_ref):
    out_ref[0] = (dot(dgate_ref[...], wg[...]) + dot(dup_ref[...], wu[...])).astype(BF16)


def weight_grads(idx_ref, *refs):
    xs, gs, (hidden, dgate, dup, gg, ug, dg) = refs[:10], refs[10:20], refs[20:]
    width = xs[0].shape[1]
    rows = xs[0].shape[0]
    for core in range(2):
        for place in range(4):
            cols = columns(idx_ref, core * 4 + place, width)
            for left, right, out in ((dgate, xs, gg), (dup, xs, ug), (hidden, gs, dg)):
                if place < 3:
                    total = dot(left[...], right[core * 5 + place][...], TN)
                else:
                    total = dot(left[: rows // 2, :], right[core * 5 + 3][...], TN)
                    total = total + dot(left[rows // 2 :, :], right[core * 5 + 4][...], TN)
                out[:, cols] = total.astype(BF16)


def call(kernel, n_in, outs, *args, flops=0):
    moved = sum(a.size * a.dtype.itemsize for a in args) + sum(o.size * o.dtype.itemsize for o in outs)
    return pl.pallas_call(
        kernel,
        grid_spec=pltpu.PrefetchScalarGridSpec(
            num_scalar_prefetch=1, grid=(), in_specs=[VMEM] * n_in, out_specs=[VMEM] * len(outs)
        ),
        out_shape=outs,
        compiler_params=PARAMS,
        cost_estimate=pl.CostEstimate(flops=flops, bytes_accessed=moved, transcendentals=0),
    )(*args)


def per_device(tokens, cotangent, gates, routing, gate_weight, up_weight, down_weight):
    tok, width = tokens.shape
    n_exp, n_y = lax.axis_size("expert"), lax.axis_size("dp")
    experts = n_exp // 2
    capacity = 2 * tok * routing.shape[1] // experts
    rows = n_exp * capacity
    part = width // n_y
    block = part // 2
    hid = gate_weight.shape[1]
    y = lax.axis_index("dp").astype(jnp.int32)
    core = (lax.axis_index("expert") % 2).astype(jnp.int32)
    near = (y + jnp.array([0, n_y - 1, 1, 2], jnp.int32)) % n_y
    idx = jnp.concatenate([2 * near + core, 2 * near + (1 - core)])
    turn = [(i, (i + 1) % n_y) for i in range(n_y)]
    back_turn = [(i, (i - 1) % n_y) for i in range(n_y)]
    swap_pairs = [(i, i ^ 1) for i in range(n_exp)]

    def right(a):
        return lax.ppermute(a, "dp", turn)

    def left(a):
        return lax.ppermute(a, "dp", back_turn)

    def swap(a):
        return lax.ppermute(a, "expert", swap_pairs)

    def exchange(a):
        return lax.all_to_all(a, "expert", split_axis=0, concat_axis=0, tiled=True)

    wg, wu, wd = gate_weight[0], up_weight[0], down_weight[0]
    routes = routing.T
    yidx = y.reshape(1)

    def build(kernel, extra, data):
        return pl.pallas_call(
            functools.partial(kernel, experts, capacity),
            grid_spec=pltpu.PrefetchScalarGridSpec(
                num_scalar_prefetch=1,
                grid=(1,),
                in_specs=[pl.BlockSpec(a.shape, lambda i, s: (0, 0)) for a in (routes, *extra)]
                + [pl.BlockSpec((tok, part), lambda i, s: (0, s[0]))],
                out_specs=pl.BlockSpec((experts, 2, capacity, block), lambda i, s: (0, 0, 0, 0)),
            ),
            out_shape=jax.ShapeDtypeStruct((experts, 2, capacity, block), BF16),
            compiler_params=PARAMS,
        )(yidx, routes, *extra, data).reshape(n_exp, capacity, block)

    def spread(a):
        own = a.reshape(rows, block)
        p, m = right(own), left(own)
        q, r = right(p[: rows // 2]), left(m[rows // 2 :])
        mine = (own, p, m, q, r)
        return mine + tuple(swap(b) for b in mine)

    xs = spread(exchange(build(build_x, (), tokens)))
    gs = spread(exchange(build(build_g, (gates,), cotangent)))

    unit = 2 * rows * hid * width
    f32_mid = jax.ShapeDtypeStruct((rows, hid), F32)
    b16_mid = jax.ShapeDtypeStruct((rows, hid), BF16)
    gate, up = call(gate_up, 12, [f32_mid] * 2, idx, *xs, wg, wu, flops=2 * unit)
    hidden, dgate, dup = call(middle, 13, [b16_mid] * 3, idx, *gs, wd, gate, up, flops=unit)

    def terms(places):
        n = len(places)
        return pl.pallas_call(
            term_block,
            grid_spec=pltpu.PrefetchScalarGridSpec(
                num_scalar_prefetch=1,
                grid=(n,),
                in_specs=[pl.BlockSpec((rows, hid), lambda i, s: (0, 0))] * 2
                + [pl.BlockSpec((hid, block), lambda i, s: (0, s[i]))] * 2,
                out_specs=pl.BlockSpec((1, rows, block), lambda i, s: (i, 0, 0)),
            ),
            out_shape=jax.ShapeDtypeStruct((n, rows, block), BF16),
            compiler_params=PARAMS,
            cost_estimate=pl.CostEstimate(
                flops=unit // 4 * n, bytes_accessed=n * rows * block * 2, transcendentals=0
            ),
        )(idx[jnp.array(places, jnp.int32)], dgate, dup, wg, wu)

    def added(*parts):
        return sum(a.astype(F32) for a in parts)

    def over_cores(place):
        both = terms([4 + place, place])
        return both[1], swap(both[0])

    h = rows // 2
    a2, b2 = over_cores(3)
    opposite = added(a2, b2).astype(BF16)
    from_left, from_right = right(opposite[:h]), left(opposite[h:])
    a, b = over_cores(2)
    ahead0 = added(a[:h], b[:h], from_left).astype(BF16)
    ahead1 = added(a[h:], b[h:]).astype(BF16)
    a, b = over_cores(1)
    behind0 = added(a[:h], b[:h]).astype(BF16)
    behind1 = added(a[h:], b[h:], from_right).astype(BF16)
    got1, got2 = right(ahead1), left(behind0)
    got0, got3 = right(ahead0), left(behind1)
    a, b = over_cores(0)
    total = jnp.concatenate(
        [
            added(a[:h], b[:h], got0, got2).astype(BF16),
            added(a[h:], b[h:], got1, got3).astype(BF16),
        ]
    )
    back = exchange(total.reshape(n_exp, capacity, block))

    grads = call(
        weight_grads,
        23,
        [jax.ShapeDtypeStruct((hid, width), BF16)] * 3,
        idx,
        *xs,
        *gs,
        hidden,
        dgate,
        dup,
        flops=3 * unit,
    )
    input_grad = pl.pallas_call(
        functools.partial(combine, experts, capacity),
        in_specs=[VMEM] * 2,
        out_specs=VMEM,
        out_shape=jax.ShapeDtypeStruct((tok, part), BF16),
        compiler_params=PARAMS,
    )(routes, back.reshape(experts, 2, capacity, block))
    return (input_grad, grads[0][None], grads[1][None], grads[2][None])


def solution(mesh):
    weights = P("expert", "dp", None)
    return jax.shard_map(
        per_device,
        mesh=mesh,
        in_specs=(P("expert", None),) * 4 + (weights,) * 3,
        out_specs=(P("expert", "dp"),) + (weights,) * 3,
        check_vma=False,
    )
```

```python
import functools
import math

import jax
import jax.numpy as jnp
from jax import lax
from jax.experimental import pallas as pl
from jax.experimental.pallas import tpu as pltpu
from jax.sharding import PartitionSpec as P

F32 = jnp.float32
BF16 = jnp.bfloat16
NT = (((1,), (1,)), ((), ()))
TN = (((0,), (0,)), ((), ()))
MIB = 1024 * 1024


def dot(a, b, dims=(((1,), (0,)), ((), ()))):
    return lax.dot_general(a, b, dims, preferred_element_type=F32)


def slot_masks(routing_ref, experts, capacity):
    tok = routing_ref.shape[1]
    ids = lax.broadcasted_iota(jnp.int32, (experts, tok), 0)
    first, second = routing_ref[0:1, :], routing_ref[1:2, :]
    hot0 = jnp.where(ids == first, 1.0, 0.0).astype(F32)
    hot1 = jnp.where(ids == second, 1.0, 0.0).astype(F32)
    row = lax.broadcasted_iota(jnp.int32, (tok, tok), 0)
    col = lax.broadcasted_iota(jnp.int32, (tok, tok), 1)
    before = jnp.where(row < col, 1.0, 0.0).astype(BF16)
    count0 = dot(hot0.astype(BF16), before)
    count1 = dot(hot1.astype(BF16), before) + jnp.sum(hot0, axis=1, keepdims=True)
    rank0 = jnp.sum(hot0 * count0, axis=0, keepdims=True).astype(jnp.int32)
    rank1 = jnp.sum(hot1 * count1, axis=0, keepdims=True).astype(jnp.int32)
    slots = lax.broadcasted_iota(jnp.int32, (experts * capacity, tok), 0)
    return (
        jnp.where(slots == first * capacity + rank0, 1.0, 0.0).astype(BF16),
        jnp.where(slots == second * capacity + rank1, 1.0, 0.0).astype(BF16),
    )


def fetch_part(whole_ref, part_ref, sem):
    part = part_ref.shape[1]
    start = pl.multiple_of(lax.axis_index("dp") * part, part)
    return pltpu.make_async_copy(whole_ref.at[:, pl.ds(start, part)], part_ref, sem)


def build_x(experts, capacity, routing_ref, tok_ref, out_ref, part_ref, sem):
    copy = fetch_part(tok_ref, part_ref, sem)
    copy.start()
    mask0, mask1 = slot_masks(routing_ref, experts, capacity)
    copy.wait()
    out_ref[...] = dot(mask0 + mask1, part_ref[...]).astype(BF16)


def build_g(experts, capacity, routing_ref, gates_ref, cot_ref, out_ref, masks_ref, part_ref, sem):
    copy = fetch_part(cot_ref, part_ref, sem)
    copy.start()
    mask0, mask1 = slot_masks(routing_ref, experts, capacity)
    masks_ref[...] = (mask0 + mask1).astype(F32).T.astype(BF16)
    gates = gates_ref[...].T
    copy.wait()
    cot = part_ref[...].astype(F32)
    scaled = dot(mask0, (gates[:, 0:1] * cot).astype(BF16))
    scaled = scaled + dot(mask1, (gates[:, 1:2] * cot).astype(BF16))
    out_ref[...] = scaled.astype(BF16)


def combine(masks_ref, *refs):
    out_ref = refs[-1]
    half = refs[0].shape[1]
    for i, back_ref in enumerate(refs[:-1]):
        out_ref[:, i * half : (i + 1) * half] = dot(masks_ref[...], back_ref[...]).astype(BF16)


def columns(near_ref, place, width):
    return pl.ds(pl.multiple_of(near_ref[place] * width, width), width)


def gate_up(near_ref, *refs):
    xs, (wg, wu, gate_ref, up_ref) = refs[:10], refs[10:]
    rows, part = xs[0].shape
    h = rows // 2
    far = columns(near_ref, 3, part)
    for core in range(2):
        for w, out_ref in ((wg, gate_ref), (wu, up_ref)):
            total = None
            for place in range(3):
                a = dot(xs[core * 5 + place][...], w[:, columns(near_ref, place, part)], NT)
                total = a if place == 0 else total + a
            for half in range(2):
                here = slice(core * rows + half * h, core * rows + (half + 1) * h)
                out_ref[here, :] = total[half * h : (half + 1) * h] + dot(xs[core * 5 + 3 + half][...], w[:, far], NT)


def first_down(near_ref, *refs):
    gs, (wd, dhid_ref) = refs[:6], refs[6:]
    rows, part = gs[0].shape
    for core in range(2):
        dhid = None
        for place in range(3):
            a = dot(gs[core * 3 + place][...], wd[:, columns(near_ref, place, part)], NT)
            dhid = a if place == 0 else dhid + a
        dhid_ref[core * rows : (core + 1) * rows, :] = dhid


def last_products(near_ref, q, r, q_other, r_other, wd, gate_ref, up_ref, dhid_ref, hidden_ref, both_ref):
    h = q.shape[0]
    for i, g in enumerate((q, r, q_other, r_other)):
        here = slice(i * h, (i + 1) * h)
        gate, up = gate_ref[here, :], up_ref[here, :]
        dhid = dhid_ref[here, :] + dot(g[...], wd[...], NT)
        sigma = jax.nn.sigmoid(gate)
        active = gate * sigma
        hidden_ref[here, :] = (active * up).astype(BF16)
        dgate = (dhid * up * sigma * (1.0 + gate * (1.0 - sigma))).astype(BF16)
        dup = (dhid * active).astype(BF16)
        both_ref[here, :] = jnp.concatenate([dgate, dup], axis=1)


def term_block(near_ref, both_ref, wg, wu, mine_ref, theirs_ref):
    rows = mine_ref.shape[0]
    weights = jnp.concatenate([wg[...], wu[...]], axis=0)
    theirs_ref[...] = dot(both_ref[rows:, :], weights).astype(BF16)
    mine_ref[...] = dot(both_ref[:rows, :], weights).astype(BF16)


def near_blocks(near_ref, both_ref, *refs):
    for i in range(2):
        term_block(near_ref, both_ref, *refs[2 * i : 2 * i + 2], *refs[4 + 2 * i : 6 + 2 * i])


def cut(near_ref, p_ref, m_ref, x_ref, g_ref):
    x_ref[...] = p_ref[...]
    g_ref[...] = m_ref[...]


def plus(*refs):
    return sum(r[...].astype(F32) for r in refs)


def add_halves(near_ref, a_ref, b_ref, lo_ref, hi_ref):
    h = lo_ref.shape[0]
    total = plus(a_ref, b_ref).astype(BF16)
    lo_ref[...] = total[:h]
    hi_ref[...] = total[h:]


def add_beside(near_ref, a_ref, b_ref, lo_ref, c_ref, d_ref, hi_ref, *outs):
    h, part = lo_ref.shape
    for i in range(2):
        cols = slice(i * part // 2, (i + 1) * part // 2)
        for a, b, extra, at, out in ((a_ref, b_ref, lo_ref, 0, outs[i]), (c_ref, d_ref, hi_ref, 1, outs[2 + i])):
            for side in range(2):
                here = slice(side * h, (side + 1) * h)
                total = a[here, cols].astype(F32) + b[here, cols].astype(F32)
                if side == at:
                    total = total + extra[:, cols].astype(F32)
                out[here, :] = total.astype(BF16)


def add_last(near_ref, *refs):
    refs[-1][...] = plus(*refs[:-1]).astype(BF16)


def nothing(*refs):
    pass


def after(a, *others):
    anywhere = pl.BlockSpec(memory_space=pl.ANY)
    return pl.pallas_call(
        nothing,
        in_specs=[anywhere] * (1 + len(others)),
        out_specs=anywhere,
        out_shape=jax.ShapeDtypeStruct(a.shape, a.dtype),
        input_output_aliases={0: 0},
        compiler_params=pltpu.CompilerParams(vmem_limit_bytes=MIB),
        cost_estimate=pl.CostEstimate(flops=0, bytes_accessed=0, transcendentals=0),
    )(a, *others)


def weight_grads(near_ref, *refs):
    xs, gs, (hidden_ref, both_ref, gg, ug, dg) = refs[:10], refs[10:20], refs[20:]
    rows, part = xs[0].shape
    h = rows // 2
    hid = gg.shape[0]
    hidden, both = hidden_ref[...].T, both_ref[...].T
    for place in range(4):
        gate_up = down = None
        for core in range(2):
            for half in range(2):
                if place < 3 and half == 1:
                    continue
                at = core * 5 + place + half
                start = core * rows + half * h
                here = slice(start, start + xs[at].shape[0])
                a, b = dot(both[:, here], xs[at][...]), dot(hidden[:, here], gs[at][...])
                gate_up, down = (a, b) if gate_up is None else (gate_up + a, down + b)
        cols = columns(near_ref, place, part)
        gg[:, cols] = gate_up[:hid].astype(BF16)
        ug[:, cols] = gate_up[hid:].astype(BF16)
        dg[:, cols] = down.astype(BF16)


def call(kernel, near, args, outs, specs=None, deps=(), spare=10, flops=0):
    specs = specs or [None] * len(args)

    def spec(a, place=None):
        one = pl.Buffered(1)
        if place is None:
            return pl.BlockSpec(a.shape, lambda i, s: (0,) * len(a.shape), pipeline_mode=one)
        if isinstance(place, str):
            return pl.BlockSpec(
                (a.shape[0], a.shape[1] // 2), lambda i, s: (0, int(place)), pipeline_mode=one
            )
        if isinstance(place, tuple):
            return pl.BlockSpec(
                (a.shape[0] // place[1], a.shape[1]), lambda i, s: (place[0], 0), pipeline_mode=one
            )
        return pl.BlockSpec((a.shape[0], a.shape[1] // 4), lambda i, s: (0, s[place]), pipeline_mode=one)

    n = len(args)
    held = sum(math.prod(b.block_shape or a.shape) * a.dtype.itemsize for a, b in zip(args, map(spec, args, specs)))
    held += sum(o.size * o.dtype.itemsize for o in outs)

    def body(near_ref, *refs):
        kernel(near_ref, *refs[:n], *refs[n + len(deps) :])

    return pl.pallas_call(
        body,
        grid_spec=pltpu.PrefetchScalarGridSpec(
            num_scalar_prefetch=1,
            grid=(1,),
            in_specs=[spec(a, p) for a, p in zip(args, specs)] + [pl.BlockSpec(memory_space=pl.ANY)] * len(deps),
            out_specs=[spec(o) for o in outs],
        ),
        out_shape=outs,
        compiler_params=pltpu.CompilerParams(vmem_limit_bytes=held + spare * MIB),
        cost_estimate=pl.CostEstimate(flops=flops, bytes_accessed=0, transcendentals=0),
    )(near, *args, *deps)


def per_device(tokens, cotangent, gates, routing, gate_weight, up_weight, down_weight):
    tok, width = tokens.shape
    n_exp, n_y = lax.axis_size("expert"), lax.axis_size("dp")
    experts = n_exp // 2
    capacity = 2 * tok * routing.shape[1] // experts
    rows = experts * capacity
    part = width // n_y
    hid = gate_weight.shape[1]
    y = lax.axis_index("dp").astype(jnp.int32)
    near = (y + jnp.array([0, n_y - 1, 1, 2], jnp.int32)) % n_y
    turn = [(i, (i + 1) % n_y) for i in range(n_y)]
    back_turn = [(i, (i - 1) % n_y) for i in range(n_y)]
    swap_pairs = [(i, i ^ 1) for i in range(n_exp)]
    same_core = [list(range(c, n_exp, 2)) for c in range(2)]

    def right(a):
        return lax.ppermute(a, "dp", turn)

    def left(a):
        return lax.ppermute(a, "dp", back_turn)

    def swap(a):
        return lax.ppermute(a, "expert", swap_pairs)

    def exchange(a):
        shape = a.shape
        a = a.reshape(experts, capacity, shape[1])
        return lax.all_to_all(
            a, "expert", split_axis=0, concat_axis=0, tiled=True, axis_index_groups=same_core
        ).reshape(shape)

    def like(shape, dtype):
        return jax.ShapeDtypeStruct(shape, dtype)

    wg, wu, wd = gate_weight[0], up_weight[0], down_weight[0]
    routes = routing.T

    block = like((rows, part), BF16)
    half_block = like((rows // 2, part), BF16)
    vmem = pl.BlockSpec(memory_space=pltpu.VMEM)

    def slots(kernel, *args, outs):
        return pl.pallas_call(
            functools.partial(kernel, experts, capacity),
            in_specs=[vmem] * (len(args) - 1) + [pl.BlockSpec(memory_space=pl.ANY)],
            out_specs=[vmem] * len(outs),
            out_shape=outs,
            scratch_shapes=[pltpu.VMEM((tok, part), BF16), pltpu.SemaphoreType.DMA],
            compiler_params=pltpu.CompilerParams(vmem_limit_bytes=60 * MIB),
            cost_estimate=pl.CostEstimate(flops=0, bytes_accessed=0, transcendentals=0),
        )(*args)

    def cut_ends(p, m, flops=0):
        return call(cut, near, (p, m), [half_block] * 2, specs=[(0, 2), (1, 2)], flops=flops)

    x_sent = slots(build_x, routes, tokens, outs=[block])[0]
    x_own = exchange(x_sent)
    g_sent, masks = slots(build_g, routes, gates.T, cotangent, outs=[block, like((tok, rows), BF16)])
    x_own = after(x_own, g_sent)
    g_own = exchange(g_sent)

    x_p, x_m = right(x_own), left(x_own)
    x_q, x_r = cut_ends(x_p, x_m, flops=5 * 10**10)
    g_own = after(g_own, x_q)
    x_q, x_r = right(x_q), left(x_r)
    xs = (x_own, x_p, x_m, x_q, x_r)
    xs += tuple(swap(a) for a in xs)
    mids = call(gate_up, near, (*xs, wg, wu), [like((2 * rows, hid), F32)] * 2)

    g_p, g_m = right(g_own), left(g_own)
    g_first = (g_own, g_p, g_m)
    g_other = tuple(swap(a) for a in g_first)
    g_q, g_r = cut_ends(g_p, g_m)
    dhid = call(first_down, near, (*g_first, *g_other, wd), [like((2 * rows, hid), F32)], deps=mids[:1])[0]
    g_q, g_r = after(right(g_q), dhid), after(left(g_r), dhid)
    g_ends = (g_q, g_r, swap(g_q), swap(g_r))
    hidden, both = call(
        last_products,
        near,
        (*g_ends, wd, *mids, dhid),
        [like((2 * rows, hid), BF16), like((2 * rows, 2 * hid), BF16)],
        specs=[None] * 4 + [3] + [None] * 3,
    )

    side = like((rows, part // 2), BF16)
    far = call(term_block, near, (both, wg, wu), [block] * 2, specs=[None, 3, 3])
    beside = call(
        near_blocks, near, (both, *(wg, wu) * 2), [block] * 4, specs=[None, 2, 2, 1, 1], deps=far[:1]
    )
    lo, hi = call(add_halves, near, (far[0], swap(far[1])), [half_block] * 2, deps=beside[:1])
    own = call(term_block, near, (both, wg, wu), [block] * 2, specs=[None, 0, 0], deps=(lo,))
    sums = call(
        add_beside,
        near,
        (beside[0], swap(beside[1]), right(lo), beside[2], swap(beside[3]), left(hi)),
        [side] * 4,
    )
    own = (own[0], swap(own[1]))

    def total(i, deps=()):
        args = (*own, right(sums[i]), left(sums[2 + i]))
        return call(add_last, near, args, [side], specs=[str(i)] * 2 + [None] * 2, deps=deps, flops=10**12)[0]

    first = total(0)
    back = [exchange(first), exchange(total(1, (first,)))]
    grads = call(
        weight_grads,
        near,
        (*xs, *g_first, *g_ends[:2], *g_other, *g_ends[2:], hidden, both),
        [like((hid, width), BF16)] * 3,
        spare=38,
        flops=10**12,
    )
    input_grad = pl.pallas_call(
        combine,
        in_specs=[vmem] * 3,
        out_specs=vmem,
        out_shape=like((tok, part), BF16),
    )(masks, *back)
    return (input_grad, grads[0][None], grads[1][None], grads[2][None])


def solution(mesh):
    weights = P("expert", "dp", None)
    return jax.shard_map(
        per_device,
        mesh=mesh,
        in_specs=(P("expert", None),) * 4 + (weights,) * 3,
        out_specs=(P("expert", "dp"),) + (weights,) * 3,
        check_vma=False,
    )
```

```python
import functools
import math

import jax
import jax.numpy as jnp
from jax import lax
from jax.experimental import pallas as pl
from jax.experimental.pallas import tpu as pltpu
from jax.sharding import PartitionSpec as P

F32 = jnp.float32
BF16 = jnp.bfloat16
NT = (((1,), (1,)), ((), ()))
TN = (((0,), (0,)), ((), ()))
MIB = 1024 * 1024


def dot(a, b, dims=(((1,), (0,)), ((), ()))):
    return lax.dot_general(a, b, dims, preferred_element_type=F32)


def slot_masks(routing_ref, experts, capacity):
    tok = routing_ref.shape[1]
    ids = lax.broadcasted_iota(jnp.int32, (experts, tok), 0)
    first, second = routing_ref[0:1, :], routing_ref[1:2, :]
    hot0 = jnp.where(ids == first, 1.0, 0.0).astype(F32)
    hot1 = jnp.where(ids == second, 1.0, 0.0).astype(F32)
    row = lax.broadcasted_iota(jnp.int32, (tok, tok), 0)
    col = lax.broadcasted_iota(jnp.int32, (tok, tok), 1)
    before = jnp.where(row < col, 1.0, 0.0).astype(BF16)
    count0 = dot(hot0.astype(BF16), before)
    count1 = dot(hot1.astype(BF16), before) + jnp.sum(hot0, axis=1, keepdims=True)
    rank0 = jnp.sum(hot0 * count0, axis=0, keepdims=True).astype(jnp.int32)
    rank1 = jnp.sum(hot1 * count1, axis=0, keepdims=True).astype(jnp.int32)
    slots = lax.broadcasted_iota(jnp.int32, (experts * capacity, tok), 0)
    return (
        jnp.where(slots == first * capacity + rank0, 1.0, 0.0).astype(BF16),
        jnp.where(slots == second * capacity + rank1, 1.0, 0.0).astype(BF16),
    )


def fetch_part(whole_ref, part_ref, sem):
    part = part_ref.shape[1]
    start = pl.multiple_of(lax.axis_index("dp") * part, part)
    return pltpu.make_async_copy(whole_ref.at[:, pl.ds(start, part)], part_ref, sem)


def build_x(experts, capacity, routing_ref, tok_ref, out_ref, part_ref, sem):
    copy = fetch_part(tok_ref, part_ref, sem)
    copy.start()
    mask0, mask1 = slot_masks(routing_ref, experts, capacity)
    copy.wait()
    out_ref[...] = dot(mask0 + mask1, part_ref[...]).astype(BF16)


def build_g(experts, capacity, routing_ref, gates_ref, cot_ref, out_ref, masks_ref, part_ref, sem):
    copy = fetch_part(cot_ref, part_ref, sem)
    copy.start()
    mask0, mask1 = slot_masks(routing_ref, experts, capacity)
    masks_ref[...] = (mask0 + mask1).astype(F32).T.astype(BF16)
    gates = gates_ref[...].T
    copy.wait()
    cot = part_ref[...].astype(F32)
    scaled = dot(mask0, (gates[:, 0:1] * cot).astype(BF16))
    scaled = scaled + dot(mask1, (gates[:, 1:2] * cot).astype(BF16))
    out_ref[...] = scaled.astype(BF16)


def combine(masks_ref, first_ref, second_ref, out_ref):
    cut = second_ref.shape[1]
    out_ref[:, cut:] = dot(masks_ref[...], first_ref[...]).astype(BF16)
    out_ref[:, :cut] = dot(masks_ref[...], second_ref[...]).astype(BF16)


def columns(near_ref, place, width):
    return pl.ds(pl.multiple_of(near_ref[place] * width, width), width)


def gate_up(near_ref, *refs):
    xs, (wg, wu, gate_ref, up_ref) = refs[:10], refs[10:]
    rows, part = xs[0].shape
    h = rows // 2
    far = columns(near_ref, 3, part)
    for core in range(2):
        for w, out_ref in ((wg, gate_ref), (wu, up_ref)):
            total = None
            for place in range(3):
                a = dot(xs[core * 5 + place][...], w[:, columns(near_ref, place, part)], NT)
                total = a if place == 0 else total + a
            for half in range(2):
                here = slice(core * rows + half * h, core * rows + (half + 1) * h)
                out_ref[here, :] = total[half * h : (half + 1) * h] + dot(xs[core * 5 + 3 + half][...], w[:, far], NT)


def first_down(near_ref, *refs):
    gs, (wd, dhid_ref) = refs[:6], refs[6:]
    rows, part = gs[0].shape
    for core in range(2):
        dhid = None
        for place in range(3):
            a = dot(gs[core * 3 + place][...], wd[:, columns(near_ref, place, part)], NT)
            dhid = a if place == 0 else dhid + a
        dhid_ref[core * rows : (core + 1) * rows, :] = dhid


def last_products(near_ref, q, r, q_other, r_other, wd, gate_ref, up_ref, dhid_ref, hidden_ref, both_ref):
    h = q.shape[0]
    for i, g in enumerate((q, r, q_other, r_other)):
        here = slice(i * h, (i + 1) * h)
        gate, up = gate_ref[here, :], up_ref[here, :]
        dhid = dhid_ref[here, :] + dot(g[...], wd[...], NT)
        sigma = jax.nn.sigmoid(gate)
        active = gate * sigma
        hidden_ref[here, :] = (active * up).astype(BF16)
        dgate = (dhid * up * sigma * (1.0 + gate * (1.0 - sigma))).astype(BF16)
        dup = (dhid * active).astype(BF16)
        both_ref[here, :] = jnp.concatenate([dgate, dup], axis=1)


def term_block(near_ref, both_ref, wg, wu, mine_ref, theirs_ref):
    rows = mine_ref.shape[0]
    weights = jnp.concatenate([wg[...], wu[...]], axis=0)
    theirs_ref[...] = dot(both_ref[rows:, :], weights).astype(BF16)
    mine_ref[...] = dot(both_ref[:rows, :], weights).astype(BF16)


def near_blocks(near_ref, both_ref, *refs):
    for i in range(2):
        term_block(near_ref, both_ref, *refs[2 * i : 2 * i + 2], *refs[4 + 2 * i : 6 + 2 * i])


def cut(near_ref, p_ref, m_ref, x_ref, g_ref):
    x_ref[...] = p_ref[...]
    g_ref[...] = m_ref[...]


def plus(*refs):
    return sum(r[...].astype(F32) for r in refs)


def add_halves(near_ref, a_ref, b_ref, lo_ref, hi_ref):
    h = lo_ref.shape[0]
    total = plus(a_ref, b_ref).astype(BF16)
    lo_ref[...] = total[:h]
    hi_ref[...] = total[h:]


def add_beside(near_ref, a_ref, b_ref, lo_ref, c_ref, d_ref, hi_ref, *outs):
    h, part = lo_ref.shape
    border = outs[1].shape[1]
    for i, cols in enumerate((slice(border, part), slice(0, border))):
        for a, b, extra, at, out in ((a_ref, b_ref, lo_ref, 0, outs[i]), (c_ref, d_ref, hi_ref, 1, outs[2 + i])):
            for side in range(2):
                here = slice(side * h, (side + 1) * h)
                total = a[here, cols].astype(F32) + b[here, cols].astype(F32)
                if side == at:
                    total = total + extra[:, cols].astype(F32)
                out[here, :] = total.astype(BF16)


def add_last(near_ref, *refs):
    refs[-1][...] = plus(*refs[:-1]).astype(BF16)


def nothing(*refs):
    pass


def after(a, *others):
    anywhere = pl.BlockSpec(memory_space=pl.ANY)
    return pl.pallas_call(
        nothing,
        in_specs=[anywhere] * (1 + len(others)),
        out_specs=anywhere,
        out_shape=jax.ShapeDtypeStruct(a.shape, a.dtype),
        input_output_aliases={0: 0},
        compiler_params=pltpu.CompilerParams(vmem_limit_bytes=MIB),
        cost_estimate=pl.CostEstimate(flops=0, bytes_accessed=0, transcendentals=0),
    )(a, *others)


def weight_grads(near_ref, *refs):
    xs, gs, (hidden_ref, both_ref, gg, ug, dg) = refs[:10], refs[10:20], refs[20:]
    rows, part = xs[0].shape
    h = rows // 2
    hid = gg.shape[0]
    hidden, both = hidden_ref[...].T, both_ref[...].T
    for place in range(4):
        gate_up = down = None
        for core in range(2):
            for half in range(2):
                if place < 3 and half == 1:
                    continue
                at = core * 5 + place + half
                start = core * rows + half * h
                here = slice(start, start + xs[at].shape[0])
                a, b = dot(both[:, here], xs[at][...]), dot(hidden[:, here], gs[at][...])
                gate_up, down = (a, b) if gate_up is None else (gate_up + a, down + b)
        cols = columns(near_ref, place, part)
        gg[:, cols] = gate_up[:hid].astype(BF16)
        ug[:, cols] = gate_up[hid:].astype(BF16)
        dg[:, cols] = down.astype(BF16)


def call(kernel, near, args, outs, specs=None, deps=(), spare=10, flops=0):
    specs = specs or [None] * len(args)

    def spec(a, place=None):
        one = pl.Buffered(1)
        if place is None:
            return pl.BlockSpec(a.shape, lambda i, s: (0,) * len(a.shape), pipeline_mode=one)
        if isinstance(place, str):
            at, wide = map(int, place.split())
            return pl.BlockSpec((a.shape[0], wide), lambda i, s: (0, at), pipeline_mode=one)
        if isinstance(place, tuple):
            return pl.BlockSpec(
                (a.shape[0] // place[1], a.shape[1]), lambda i, s: (place[0], 0), pipeline_mode=one
            )
        return pl.BlockSpec((a.shape[0], a.shape[1] // 4), lambda i, s: (0, s[place]), pipeline_mode=one)

    n = len(args)
    held = sum(math.prod(b.block_shape or a.shape) * a.dtype.itemsize for a, b in zip(args, map(spec, args, specs)))
    held += sum(o.size * o.dtype.itemsize for o in outs)

    def body(near_ref, *refs):
        kernel(near_ref, *refs[:n], *refs[n + len(deps) :])

    return pl.pallas_call(
        body,
        grid_spec=pltpu.PrefetchScalarGridSpec(
            num_scalar_prefetch=1,
            grid=(1,),
            in_specs=[spec(a, p) for a, p in zip(args, specs)] + [pl.BlockSpec(memory_space=pl.ANY)] * len(deps),
            out_specs=[spec(o) for o in outs],
        ),
        out_shape=outs,
        compiler_params=pltpu.CompilerParams(vmem_limit_bytes=held + spare * MIB),
        cost_estimate=pl.CostEstimate(flops=flops, bytes_accessed=0, transcendentals=0),
    )(near, *args, *deps)


def per_device(tokens, cotangent, gates, routing, gate_weight, up_weight, down_weight):
    tok, width = tokens.shape
    n_exp, n_y = lax.axis_size("expert"), lax.axis_size("dp")
    experts = n_exp // 2
    capacity = 2 * tok * routing.shape[1] // experts
    rows = experts * capacity
    part = width // n_y
    hid = gate_weight.shape[1]
    y = lax.axis_index("dp").astype(jnp.int32)
    near = (y + jnp.array([0, n_y - 1, 1, 2], jnp.int32)) % n_y
    turn = [(i, (i + 1) % n_y) for i in range(n_y)]
    back_turn = [(i, (i - 1) % n_y) for i in range(n_y)]
    swap_pairs = [(i, i ^ 1) for i in range(n_exp)]
    same_core = [list(range(c, n_exp, 2)) for c in range(2)]

    def right(a):
        return lax.ppermute(a, "dp", turn)

    def left(a):
        return lax.ppermute(a, "dp", back_turn)

    def swap(a):
        return lax.ppermute(a, "expert", swap_pairs)

    def exchange(a):
        shape = a.shape
        a = a.reshape(experts, capacity, shape[1])
        return lax.all_to_all(
            a, "expert", split_axis=0, concat_axis=0, tiled=True, axis_index_groups=same_core
        ).reshape(shape)

    def like(shape, dtype):
        return jax.ShapeDtypeStruct(shape, dtype)

    wg, wu, wd = gate_weight[0], up_weight[0], down_weight[0]
    routes = routing.T

    block = like((rows, part), BF16)
    half_block = like((rows // 2, part), BF16)
    vmem = pl.BlockSpec(memory_space=pltpu.VMEM)

    def slots(kernel, *args, outs):
        return pl.pallas_call(
            functools.partial(kernel, experts, capacity),
            in_specs=[vmem] * (len(args) - 1) + [pl.BlockSpec(memory_space=pl.ANY)],
            out_specs=[vmem] * len(outs),
            out_shape=outs,
            scratch_shapes=[pltpu.VMEM((tok, part), BF16), pltpu.SemaphoreType.DMA],
            compiler_params=pltpu.CompilerParams(vmem_limit_bytes=60 * MIB),
            cost_estimate=pl.CostEstimate(flops=0, bytes_accessed=0, transcendentals=0),
        )(*args)

    def cut_ends(p, m, flops=0):
        return call(cut, near, (p, m), [half_block] * 2, specs=[(0, 2), (1, 2)], flops=flops)

    x_sent = slots(build_x, routes, tokens, outs=[block])[0]
    x_own = exchange(x_sent)
    g_sent, masks = slots(build_g, routes, gates.T, cotangent, outs=[block, like((tok, rows), BF16)])
    x_own = after(x_own, g_sent)
    g_own = exchange(g_sent)

    x_p, x_m = right(x_own), left(x_own)
    x_q, x_r = cut_ends(x_p, x_m, flops=5 * 10**10)
    g_own = after(g_own, x_q)
    x_q, x_r = right(x_q), left(x_r)
    xs = (x_own, x_p, x_m, x_q, x_r)
    xs += tuple(swap(a) for a in xs)
    mids = call(gate_up, near, (*xs, wg, wu), [like((2 * rows, hid), F32)] * 2)

    g_p, g_m = right(g_own), left(g_own)
    g_first = (g_own, g_p, g_m)
    g_other = tuple(swap(a) for a in g_first)
    g_q, g_r = cut_ends(g_p, g_m)
    dhid = call(first_down, near, (*g_first, *g_other, wd), [like((2 * rows, hid), F32)], deps=mids[:1])[0]
    g_q, g_r = after(right(g_q), dhid), after(left(g_r), dhid)
    g_ends = (g_q, g_r, swap(g_q), swap(g_r))
    hidden, both = call(
        last_products,
        near,
        (*g_ends, wd, *mids, dhid),
        [like((2 * rows, hid), BF16), like((2 * rows, 2 * hid), BF16)],
        specs=[None] * 4 + [3] + [None] * 3,
    )

    narrow = part // 4
    sides = [like((rows, narrow), BF16), like((rows, part - narrow), BF16)]
    halves = [f"3 {narrow}", f"0 {part - narrow}"]
    far = call(term_block, near, (both, wg, wu), [block] * 2, specs=[None, 3, 3])
    beside = call(
        near_blocks, near, (both, *(wg, wu) * 2), [block] * 4, specs=[None, 2, 2, 1, 1], deps=far[:1]
    )
    lo, hi = call(add_halves, near, (far[0], swap(far[1])), [half_block] * 2, deps=beside[:1])
    own = call(term_block, near, (both, wg, wu), [block] * 2, specs=[None, 0, 0], deps=(lo,))
    sums = call(
        add_beside,
        near,
        (beside[0], swap(beside[1]), right(lo), beside[2], swap(beside[3]), left(hi)),
        sides * 2,
    )
    own = (own[0], swap(own[1]))

    def total(i, deps=()):
        args = (*own, right(sums[i]), left(sums[2 + i]))
        return call(add_last, near, args, sides[i : i + 1], specs=[halves[i]] * 2 + [None] * 2, deps=deps, flops=10**12)[0]

    first = total(0)
    back = [exchange(first), exchange(total(1, (first,)))]
    grads = call(
        weight_grads,
        near,
        (*xs, *g_first, *g_ends[:2], *g_other, *g_ends[2:], hidden, both),
        [like((hid, width), BF16)] * 3,
        spare=38,
        flops=10**12,
    )
    input_grad = pl.pallas_call(
        combine,
        in_specs=[vmem] * 3,
        out_specs=vmem,
        out_shape=like((tok, part), BF16),
    )(masks, *back)
    return (input_grad, grads[0][None], grads[1][None], grads[2][None])


def solution(mesh):
    weights = P("expert", "dp", None)
    return jax.shard_map(
        per_device,
        mesh=mesh,
        in_specs=(P("expert", None),) * 4 + (weights,) * 3,
        out_specs=(P("expert", "dp"),) + (weights,) * 3,
        check_vma=False,
    )
```
